32 devices in a mesh: gx: 4 (over y, x), gy: 8 (over z, core).
Axes of the slice: x: 2, y: 2, z: 4, core: 2. Of those that a mesh axis runs over, the one named last changes fastest.
Arguments:
- gas_pos: float32 [512, 3, 128], P(('gx', 'gy')), may hold values from -6 to 6
- gas_vel: float32 [512, 3, 128], P(('gx', 'gy')), may hold values from -4 to 4
- gas_mass: float32 [512, 128], P(('gx', 'gy')), may hold values from 0.5 to 2
- gas_smooth: float32 [512, 128], P(('gx', 'gy')), may hold values from 0.3 to 1
- gas_energy: float32 [512, 128], P(('gx', 'gy')), may hold values from 1 to 3
- gas_metals: float32 [512, 16, 128], P(('gx', 'gy')), may hold values from 0.001 to 0.05
- gas_bins: int32 [512], P(('gx', 'gy')), may hold values from 0 to 2
- gas_nbr_dev: int32 [512, 8], P(('gx', 'gy')), may hold values from 0 to 31, all different within a row; in each aligned block of 16 rows (0 to 15, 16 to 31, ...) at most 8 rows name the same one
- gas_nbr_slot: int32 [512, 8], P(('gx', 'gy')), may hold values from 0 to 15
- star_pos: float32 [256, 3, 128], P(('gx', 'gy')), may hold values from -2.5 to 2.5
- star_vel: float32 [256, 3, 128], P(('gx', 'gy')), may hold values from -3 to 3
- star_radius: float32 [256, 128], P(('gx', 'gy')), may hold values from 0.5 to 1.5
- star_mdot: float32 [256, 128], P(('gx', 'gy')), may hold values from 3 to 24
- star_edot: float32 [256, 128], P(('gx', 'gy')), may hold values from 1 to 8
- star_yields: float32 [256, 16, 128], P(('gx', 'gy')), may hold values from 0.02 to 0.2
- star_ovl_dev: int32 [256, 16], P(('gx', 'gy')), may hold values from 0 to 31, all different within a row; in each aligned block of 8 rows (0 to 7, 8 to 15, ...) at most 8 rows name the same one
- star_ovl_slot: int32 [256, 16], P(('gx', 'gy')), may hold values from 0 to 15
Outputs:
- final_pos: float32 [512, 3, 128], P(('gx', 'gy'))
- final_vel: float32 [512, 3, 128], P(('gx', 'gy'))
- final_mass: float32 [512, 128], P(('gx', 'gy'))
- final_energy: float32 [512, 128], P(('gx', 'gy'))
- final_metals: float32 [512, 16, 128], P(('gx', 'gy'))
The draws below stay inside these ranges and needn't reach their ends.
Inputs may be any that keep to these rules, and one draw needn't show every extreme that they name: `gas_nbr_dev`: each gas block names 8 different devices; among the gas blocks of one device no device is named more than 8 times, and some device exactly 8 times. `star_ovl_dev`: each star block names 16 different devices; among the star blocks of one device no device is named more than 8 times, and some device exactly 8 times.
All inputs are finite; a program needn't handle non-finite values.
Results may differ from the reference program's by a relative error of at most 0.00011.
Values sent between devices are 32-bit elements; how exact they have to be, the bound alone decides.
No kernel may reach another device: no remote copies, remote signals or barrier semaphores. Data moves between devices by JAX's collectives and lax.ppermute only.
A program may use at most 64 MiB of HBM per device.

```python
import math
import jax
import jax.numpy as jnp
import numpy as np
from jax import lax

BLOCK = 128
YIELDS = 16
GB_DEV = 16
SB_DEV = 8
K = 8
L = 16
SUBSTEPS = 4
PEERS = 32
CAP = 8
CAPS = 8
NG = 512
NS = 256


def draw_gas_bins(key, part):
    key_device, key_block = jax.random.split(key)
    device_level = jax.random.randint(key_device, (NG // GB_DEV,), 0, 3)
    block_level = jax.random.randint(key_block, (NG,), 0, 2)
    return jnp.minimum(jnp.repeat(device_level, GB_DEV) + block_level, 2).astype(jnp.int32)


def touch_ends(values, stream_key, smallest, largest):
    longest = values.shape.index(max(values.shape))
    spots = []
    for shift in (0, 1):
        where = [jax.random.randint(jax.random.fold_in(stream_key, axis), (), 0, length) for axis, length in enumerate(values.shape)]
        where[longest] = (where[longest] + shift) % values.shape[longest]
        spots.append(tuple(where))
    return values.at[spots[0]].set(smallest).at[spots[1]].set(largest)


def block_scale(stream_key, shape, shards, low, top_value):
    level = 1.0
    for axis_at, shards_of in shards:
        draws = jax.random.uniform(jax.random.fold_in(jax.random.fold_in(stream_key, 6), axis_at), (shards_of,), jnp.float32, low / len(shards), top_value / len(shards))
        level = level * jnp.repeat(jnp.exp(draws), shape[axis_at] // shards_of).reshape((-1,) + (1,) * (len(shape) - 1 - axis_at))
    return level


def deal_out(key, own, number, rows, count, top, bound, lean):
    ranking = jax.random.permutation(key, count)
    heavy_load, ordinary = load_shares(count, rows * top, bound, lean, True), load_shares(count, rows * top, bound, lean, False)
    places = jnp.arange(count)

    def named(lengths, offset_by):
        used = int((lengths > 0).sum())
        fixed = max(1, used // 4)
        passed = fixed + (places - fixed + offset_by * (used - fixed)) % max(1, count - fixed)
        return jnp.zeros((count,), jnp.int32).at[ranking[jnp.where(places < fixed, places, passed)]].set(jnp.asarray(lengths, jnp.int32))

    lengths = jnp.where(number % 4 == 0, named(heavy_load, number // 4), named(ordinary, number - number // 4 - 1))
    mixed = jax.random.permutation(jax.random.fold_in(own, 3), count)
    source_of, receiver = mixed[0:count // 2 * 2:2], mixed[1:count // 2 * 2:2]
    slack = jnp.minimum(lengths[source_of] - 1, bound - lengths[receiver]) // 2
    slack = jnp.where((source_of == ranking[0]) | (receiver == ranking[0]) | (lengths[receiver] == 0), 0, jnp.maximum(slack, 0))
    passed = jax.random.randint(jax.random.fold_in(own, 4), (count // 2,), 0, 1 << 20) % (slack + 1)
    lengths = lengths.at[source_of].add(-passed).at[receiver].add(passed)
    items = jnp.searchsorted(jnp.cumsum(lengths), jnp.arange(rows * top), side="right").astype(jnp.int32)
    table = items.reshape(top, rows).T
    table = table[jax.random.permutation(jax.random.fold_in(own, 1), rows)]
    offset_by = jax.random.randint(jax.random.fold_in(own, 2), (rows, 1), 0, top)
    return jnp.take_along_axis(table, (jnp.arange(top)[None, :] + offset_by) % top, axis=1)


def load_shares(amount, total, reach, skew, full):
    portions = [(1 << 20) // math.isqrt(standing ** skew) + 1 for standing in range(1, amount + 1)]
    largest = reach if full else min(reach, max(-(-total // amount), total * portions[0] // sum(portions)))
    least = 1 if total - largest >= amount - 1 else 0
    counts, spare = [largest] + [least] * (amount - 1), total - largest - least * (amount - 1)
    while spare > 0:
        free = [i for i in range(1, amount) if counts[i] < largest] or [i for i in range(1, amount) if counts[i] < reach]
        mass, remaining = sum([portions[i] for i in free]), spare
        for i in free:
            more = min(reach - counts[i], max(1, remaining * portions[i] // mass), spare)
            counts[i] = counts[i] + more
            spare = spare - more
    return np.array(counts)


def normal_values(key, dims, width, bound, cuts=(), kind=jnp.bfloat16):
    drawn = width * jax.random.normal(key, dims, jnp.float32)
    if cuts:
        drawn = drawn * block_scale(key, dims, cuts, -0.22, 0.18)
    return jnp.clip(drawn, -bound, bound).astype(kind)


def setup_inputs(seed: int = 0) -> dict:
    key_list = jax.random.split(jax.random.key(seed), 18)
    gas_pos = normal_values(key_list[0], (NG, 3, BLOCK), 1.0, 6.0, ((0, 32),), jnp.float32)
    gas_vel = normal_values(key_list[1], (NG, 3, BLOCK), 1.2, 4.0, ((0, 32),), jnp.float32)
    gas_mass = jnp.clip(jnp.exp(math.log(2.0) - 1.3862944 * jax.random.uniform(key_list[2], (NG, BLOCK), jnp.float32) ** block_scale(key_list[2], (NG, BLOCK), ((0, 32),), -0.2, 0.2)), 0.5, 2.0)
    gas_smooth = jnp.clip(jnp.exp(math.log(1.0) - 1.2039728 * jax.random.uniform(key_list[3], (NG, BLOCK), jnp.float32) ** block_scale(key_list[3], (NG, BLOCK), ((0, 32),), -0.2, 0.2)), 0.3, 1.0)
    gas_energy = jnp.clip(1.0 + 2.0 * jax.random.uniform(key_list[4], (NG, BLOCK), jnp.float32) ** block_scale(key_list[4], (NG, BLOCK), ((0, 32),), -0.2, 0.2), 1.0, 3.0)
    gas_metals = jnp.clip(jnp.exp(math.log(0.05) - 3.912023 * jax.random.uniform(key_list[5], (NG, YIELDS, BLOCK), jnp.float32) ** block_scale(key_list[5], (NG, YIELDS, BLOCK), ((0, 32),), -0.2, 0.2)), 0.001, 0.05)
    gas_bins = draw_gas_bins(jax.random.fold_in(key_list[17], 71), 0)
    gas_nbr_dev_keys = jax.random.split(jax.random.fold_in(key_list[7], 1), NG // GB_DEV)
    gas_nbr_dev_turns = jax.random.permutation(jax.random.fold_in(key_list[7], 3), NG // GB_DEV)
    gas_nbr_dev = jax.vmap(lambda own, number: deal_out(jax.random.fold_in(key_list[7], 2), own, number, GB_DEV, PEERS, K, CAP, 2))(gas_nbr_dev_keys, gas_nbr_dev_turns).reshape((NG, K))
    gas_nbr_slot = touch_ends(jax.random.randint(key_list[8], (NG, K), 0, GB_DEV), jax.random.fold_in(key_list[8], 1), 0, GB_DEV - 1).astype(jnp.int32)
    star_pos = normal_values(key_list[9], (NS, 3, BLOCK), 0.8, 2.5, ((0, 32),), jnp.float32)
    star_vel = normal_values(key_list[10], (NS, 3, BLOCK), 0.5, 3.0, ((0, 32),), jnp.float32)
    star_radius = jnp.clip(jnp.exp(math.log(1.5) - 1.0986123 * jax.random.uniform(key_list[11], (NS, BLOCK), jnp.float32) ** block_scale(key_list[11], (NS, BLOCK), ((0, 32),), -0.2, 0.2)), 0.5, 1.5)
    star_mdot = jnp.clip(jnp.exp(math.log(24.0) - 2.0794415 * jax.random.uniform(key_list[12], (NS, BLOCK), jnp.float32) ** block_scale(key_list[12], (NS, BLOCK), ((0, 32),), -0.2, 0.2)), 3.0, 24.0)
    star_edot = jnp.clip(jnp.exp(math.log(8.0) - 2.0794415 * jax.random.uniform(key_list[13], (NS, BLOCK), jnp.float32) ** block_scale(key_list[13], (NS, BLOCK), ((0, 32),), -0.2, 0.2)), 1.0, 8.0)
    star_yields = jnp.clip(jnp.exp(math.log(0.2) - 2.3025851 * jax.random.uniform(key_list[14], (NS, YIELDS, BLOCK), jnp.float32) ** block_scale(key_list[14], (NS, YIELDS, BLOCK), ((0, 32),), -0.2, 0.2)), 0.02, 0.2)
    star_ovl_dev_keys = jax.random.split(jax.random.fold_in(key_list[15], 1), NS // SB_DEV)
    star_ovl_dev_turns = jax.random.permutation(jax.random.fold_in(key_list[15], 3), NS // SB_DEV)
    star_ovl_dev = jax.vmap(lambda own, number: deal_out(jax.random.fold_in(key_list[15], 2), own, number, SB_DEV, PEERS, L, CAPS, 2))(star_ovl_dev_keys, star_ovl_dev_turns).reshape((NS, L))
    star_ovl_slot = touch_ends(jax.random.randint(key_list[16], (NS, L), 0, GB_DEV), jax.random.fold_in(key_list[16], 1), 0, GB_DEV - 1).astype(jnp.int32)
    return {"gas_pos": gas_pos, "gas_vel": gas_vel, "gas_mass": gas_mass, "gas_smooth": gas_smooth, "gas_energy": gas_energy, "gas_metals": gas_metals, "gas_bins": gas_bins, "gas_nbr_dev": gas_nbr_dev, "gas_nbr_slot": gas_nbr_slot, "star_pos": star_pos, "star_vel": star_vel, "star_radius": star_radius, "star_mdot": star_mdot, "star_edot": star_edot, "star_yields": star_yields, "star_ovl_dev": star_ovl_dev, "star_ovl_slot": star_ovl_slot}


KERNEL_NORM = 0.1795871221251666
GAMMA_LESS = 0.6666666666666666
TIME_STEP = 0.05
COOL_RATE = 0.4
ENERGY_FLOOR = 0.2

def kernel(dist_sq, smooth):
    return KERNEL_NORM * jnp.exp(-dist_sq / (smooth * smooth)) / (smooth * smooth * smooth)

def geometry(own_pos, far_pos):
    offset = own_pos[None, :, :, None] - far_pos[:, :, None, :]
    return (offset, lax.optimization_barrier(jnp.sum(offset * offset, axis=1)))

def block_density(own_pos, own_smooth, far_pos, far_mass):
    offset, dist_sq = geometry(own_pos, far_pos)
    weight = kernel(dist_sq, own_smooth[None, :, None])
    return lax.optimization_barrier(jnp.sum(far_mass[:, None, :] * weight, axis=(0, 2)))

def block_force(own_pos, own_vel, own_smooth, own_term, far_pos, far_vel, far_mass, far_smooth, far_term):
    offset, dist_sq = geometry(own_pos, far_pos)
    own_width = own_smooth[None, :, None]
    far_width = far_smooth[:, None, :]
    own_grad = 2.0 * kernel(dist_sq, own_width) / (own_width * own_width)
    far_grad = 2.0 * kernel(dist_sq, far_width) / (far_width * far_width)
    coupling = far_mass[:, None, :] * (own_term[None, :, None] * own_grad + far_term[:, None, :] * far_grad)
    acceleration = lax.optimization_barrier(jnp.sum(coupling[:, None] * offset, axis=(0, 3)))
    velocity_gap = own_vel[None, :, :, None] - far_vel[:, :, None, :]
    converge = lax.optimization_barrier(jnp.sum(velocity_gap * offset, axis=1))
    heating = -own_term * lax.optimization_barrier(jnp.sum(far_mass[:, None, :] * own_grad * converge, axis=(0, 2)))
    return (acceleration, heating)

def star_deposit(star_now, star_reach, star_rate, star_power, star_speed, star_yield, gas_near):
    gas_place = gas_near[:, 0:3]
    gas_width = gas_near[:, 3]
    offset = star_now[None, :, :, None] - gas_place[:, :, None, :]
    dist_sq = lax.optimization_barrier(jnp.sum(offset * offset, axis=1))
    width_sq = gas_width[:, None, :] * gas_width[:, None, :]
    solid = 0.5 * (1.0 - jnp.sqrt(dist_sq) / jnp.sqrt(dist_sq + width_sq))
    omega = solid * jnp.exp(-dist_sq / (star_reach[None, :, None] * star_reach[None, :, None]))
    total = lax.optimization_barrier(jnp.sum(omega, axis=(0, 2)))
    share = omega / total[None, :, None]
    ejecta = star_rate * TIME_STEP
    payload = jnp.concatenate([ejecta[None], ejecta[None] * star_speed, (star_power * TIME_STEP)[None], ejecta[None] * star_yield], axis=0)
    return jnp.einsum('qs,lsg->lqg', payload, share, precision=lax.Precision.HIGHEST)

def absorb(gas_mass_now, gas_vel_now, gas_heat, gas_metal, deposit):
    new_mass = gas_mass_now + deposit[:, 0]
    new_vel = (gas_mass_now[:, None] * gas_vel_now + deposit[:, 1:4]) / new_mass[:, None]
    new_energy = (gas_mass_now * gas_heat + deposit[:, 4]) / new_mass
    new_metal = gas_metal + deposit[:, 5:]
    return (new_mass, new_vel, new_energy, new_metal)

def cooling(energy_now, density):
    return ENERGY_FLOOR + (energy_now - ENERGY_FLOOR) * jnp.exp(-TIME_STEP * COOL_RATE * density)

def grouped(func_body, *arrays):
    total_rows = arrays[0].shape[0]
    group_size = min(16, total_rows)
    shaped = tuple((member.reshape((total_rows // group_size, group_size) + member.shape[1:]) for member in arrays))
    result = lax.map(lambda inputs: jax.vmap(func_body)(*inputs), shaped)
    return jax.tree.map(lambda output: output.reshape((total_rows,) + output.shape[2:]), result)

def density_of(own_block, around):
    return block_density(own_block[0:3], own_block[7], around[:, 0:3], around[:, 6])

def force_of(own_block, around, term_own, term_near):
    return block_force(own_block[0:3], own_block[3:6], own_block[7], term_own, around[:, 0:3], around[:, 3:6], around[:, 6], around[:, 7], term_near)

def reference(gas_pos, gas_vel, gas_mass, gas_smooth, gas_energy, gas_metals, gas_bins, gas_nbr_dev, gas_nbr_slot, star_pos, star_vel, star_radius, star_mdot, star_edot, star_yields, star_ovl_dev, star_ovl_slot):
    total_blocks = gas_pos.shape[0]
    near_ids = jnp.concatenate([jnp.arange(total_blocks, dtype=jnp.int32)[:, None], (gas_nbr_dev * GB_DEV + gas_nbr_slot).astype(jnp.int32)], axis=1)
    star_ids = (star_ovl_dev * GB_DEV + star_ovl_slot).astype(jnp.int32).reshape(-1)
    period = jnp.where(gas_bins == 0, 1, jnp.where(gas_bins == 1, 2, 4)).astype(jnp.int32)
    position, velocity, masses, energy, metals = (gas_pos, gas_vel, gas_mass, gas_energy, gas_metals)
    for substep in range(SUBSTEPS):
        gas_state = jnp.concatenate([position, velocity, masses[:, None], gas_smooth[:, None], energy[:, None]], axis=1)
        near_state = gas_state[near_ids]
        density = grouped(density_of, gas_state, near_state)
        own_term = GAMMA_LESS * energy / density
        near_term = own_term[near_ids]
        acceleration, heating = grouped(force_of, gas_state, near_state, own_term, near_term)
        active = (substep % period == 0).astype(jnp.float32)
        kick_time = active * TIME_STEP * period.astype(jnp.float32)
        velocity = velocity + kick_time[:, None, None] * acceleration
        energy = energy + kick_time[:, None] * heating
        position = position + TIME_STEP * velocity
        star_now = star_pos + (substep + 1) * TIME_STEP * star_vel
        gas_reach = jnp.concatenate([position, gas_smooth[:, None]], axis=1)[star_ids]
        gas_reach = gas_reach.reshape(star_pos.shape[0], star_ovl_dev.shape[1], 4, gas_reach.shape[-1])
        star_parts = grouped(star_deposit, star_now, star_radius, star_mdot, star_edot, star_vel, star_yields, gas_reach)
        deposit = jnp.zeros((total_blocks, star_parts.shape[2], star_parts.shape[3]), jnp.float32).at[star_ids].add(star_parts.reshape((-1,) + star_parts.shape[2:]))
        energy = cooling(energy, density)
        masses, velocity, energy, metals = absorb(masses, velocity, energy, metals, deposit)
    return (position, velocity, masses, energy, metals)
```

```python
import jax
import jax.numpy as jnp
from jax import lax
from jax.experimental import pallas as pl
from jax.experimental.pallas import tpu as pltpu
from jax.sharding import PartitionSpec as P

SUBSTEPS = 4
KERNEL_NORM = 0.1795871221251666
GAMMA_LESS = 0.6666666666666666
TIME_STEP = 0.05
COOL_RATE = 0.4
ENERGY_FLOOR = 0.2
LOG2E = 1.4426950408889634
AXES = ("gx", "gy")
F32 = jnp.float32
BF16 = jnp.bfloat16
UNROLL = 4
VMEM = pl.BlockSpec(memory_space=pltpu.VMEM)
SMEM = pl.BlockSpec(memory_space=pltpu.SMEM)
PARAMS = pltpu.CompilerParams(vmem_limit_bytes=48 * 1024 * 1024)


def call(body, outs, ins, scratch=(), smem_outs=()):
    return pl.pallas_call(
        body,
        out_shape=[jax.ShapeDtypeStruct(shape, dtype) for shape, dtype in outs],
        in_specs=ins,
        out_specs=[SMEM if at in smem_outs else VMEM for at in range(len(outs))],
        scratch_shapes=list(scratch),
        compiler_params=PARAMS,
    )


def swap(payload):
    return lax.all_to_all(payload, AXES, split_axis=0, concat_axis=0, tiled=True)


def row_of(ref, at):
    return ref[pl.ds(at, 1), :]


def rows8(*rows):
    place = lax.broadcasted_iota(jnp.int32, (8, 128), 0)
    out = jnp.zeros((8, 128), F32)
    for at, row in enumerate(rows):
        out = jnp.where(place == at, row, out)
    return out


def split3(value):
    first = value.astype(BF16).astype(F32)
    rest = value - first
    second = rest.astype(BF16).astype(F32)
    third = (rest - second).astype(BF16).astype(F32)
    return first, second, third


def far_side(value):
    a, b, c = split3(value)
    return jnp.concatenate([a, a, b, b, a, c], axis=0).astype(BF16)


def near_side(value):
    a, b, c = split3(value)
    return jnp.concatenate([a, b, a, b, c, a], axis=0).T.astype(BF16)


def weights(value):
    a, b, c = split3(value)
    packed = jnp.concatenate([a, b, c, jnp.zeros_like(a)], axis=0).astype(BF16)
    return jnp.concatenate([packed, packed], axis=1)


def two_halves(value):
    first = value.astype(BF16)
    second = (value - first.astype(F32)).astype(BF16)
    return jnp.concatenate([first, second], axis=1)


def inner(left, right):
    return lax.dot_general(left, right, (((1,), (1,)), ((), ())), preferred_element_type=F32)


def outer(left, right):
    return lax.dot_general(left, right, (((1,), (0,)), ((), ())), preferred_element_type=F32)


def norm_sq(x, y, z):
    return x * x + y * y + z * z


def plan_kernel(peers, cap, sb, neighbours, entries):
    span = cap + sb

    def body(gas_dev, gas_slot, star_dev, star_slot, req, place, count):
        def clear(at, _):
            req[at] = -1
            return 0

        def clear_count(at, _):
            count[at] = 0
            return 0

        lax.fori_loop(0, peers * span, clear, 0, unroll=8)
        lax.fori_loop(0, peers, clear_count, 0, unroll=8)

        def gas(at, _):
            dev = gas_dev[at]
            used = count[dev]
            count[dev] = used + 1
            req[dev * span + used] = gas_slot[at]
            place[at] = dev * cap + used
            return 0

        def star(at, _):
            req[star_dev[at] * span + cap + at // entries] = star_slot[at]
            return 0

        lax.fori_loop(0, gas_dev.shape[0], gas, 0, unroll=4)
        lax.fori_loop(0, star_dev.shape[0], star, 0, unroll=4)

    return body


def list_kernel(peers, cap, sb, nb):
    span = cap + sb

    def body(asked, pick, list_c, list_slot, list_out, number):
        def picks(at, _):
            pick[at] = jnp.maximum(asked[(at // cap) * span + at % cap], 0)
            return 0

        lax.fori_loop(0, peers * cap, picks, 0, unroll=8)

        def stars(at, used):
            slot = asked[(at // sb) * span + cap + at % sb]
            list_c[used] = at
            list_slot[used] = slot
            list_out[used] = at
            return used + jnp.where(slot >= 0, 1, 0)

        used = lax.fori_loop(0, peers * sb, stars, 0, unroll=4)
        for extra in range(UNROLL):
            list_c[used + extra] = 0
            list_slot[used + extra] = nb
            list_out[used + extra] = peers * sb
        number[0] = (used + UNROLL - 1) // UNROLL

    return body


def send_rows(pick, out, source, width):
    total = out.shape[0] // width

    def one(at, _):
        slot = pick[at]
        for f in range(width):
            out[pl.ds(at * width + f, 1), :] = source(slot, f)
        return 0

    lax.fori_loop(0, total, one, 0, unroll=8)


def start_kernel(pick, pos, vel, mass, smooth, send_pos, send_vel, send_mass, send_smooth):
    send_rows(pick, send_pos, lambda slot, f: pos[slot, f : f + 1, :], 3)
    send_rows(pick, send_vel, lambda slot, f: vel[slot, f : f + 1, :], 3)
    send_rows(pick, send_mass, lambda slot, f: row_of(mass, slot), 1)
    send_rows(pick, send_smooth, lambda slot, f: row_of(smooth, slot), 1)


def density_kernel(neighbours):
    def body(place, pick, pos, vel, mass, smooth, energy, far_pos, far_vel, far_mass, sums, term, gain, density, send_gain):
        def block(b, _):
            x, y, z = (pos[b, f : f + 1, :] for f in range(3))
            h = row_of(smooth, b)
            scale = LOG2E / (h * h)
            near = near_side(
                rows8(2.0 * scale * x, 2.0 * scale * y, 2.0 * scale * z, -scale, -scale * norm_sq(x, y, z))
            )

            def pair(px, py, pz, vx, vy, vz, m):
                far = far_side(rows8(px, py, pz, norm_sq(px, py, pz), 1.0))
                reach = jnp.exp2(outer(near, far))
                load = rows8(
                    m, m * px, m * py, m * pz, m * vx, m * vy, m * vz, m * (px * vx + py * vy + pz * vz)
                )
                return inner(weights(load), two_halves(reach))

            total = pair(x, y, z, *(vel[b, f : f + 1, :] for f in range(3)), row_of(mass, b))
            for k in range(neighbours):
                at = place[b * neighbours + k]
                total = total + pair(
                    *(row_of(far_pos, at * 3 + f) for f in range(3)),
                    *(row_of(far_vel, at * 3 + f) for f in range(3)),
                    row_of(far_mass, at),
                )
            total = total[0:8] + total[8:16] + total[16:24]
            sums[b] = total
            dense = KERNEL_NORM * total[0:1] / (h * h * h)
            density[pl.ds(b, 1), :] = dense
            own = GAMMA_LESS * row_of(energy, b) / dense
            term[pl.ds(b, 1), :] = own
            gain[pl.ds(b, 1), :] = row_of(mass, b) * own * ((2.0 * KERNEL_NORM) / (h * h * h * h * h))
            return 0

        lax.fori_loop(0, pos.shape[0], block, 0)
        send_rows(pick, send_gain, lambda slot, f: row_of(gain, slot), 1)

    return body


def force_kernel(neighbours, substep):
    def body(
        place, pick, bins, pos, vel, smooth, energy, term, gain, sums, far_pos, far_smooth, far_gain,
        new_pos, new_vel, new_energy, send_pos,
    ):
        def block(b, _):
            period = jnp.left_shift(1, bins[b])
            active = (substep & (period - 1)) == 0
            x, y, z = (pos[b, f : f + 1, :] for f in range(3))
            u, v, w = (vel[b, f : f + 1, :] for f in range(3))

            @pl.when(active)
            def _():
                h = row_of(smooth, b)
                own = row_of(term, b)
                near = near_side(rows8(2.0 * x, 2.0 * y, 2.0 * z, -1.0, -norm_sq(x, y, z)))

                def pair(px, py, pz, width, push):
                    scale = LOG2E / (width * width)
                    far = far_side(rows8(scale * px, scale * py, scale * pz, scale * norm_sq(px, py, pz), scale))
                    reach = jnp.exp2(outer(near, far))
                    load = rows8(push, push * px, push * py, push * pz)
                    return inner(weights(load), two_halves(reach))

                total = pair(x, y, z, h, row_of(gain, b))

                for k in range(neighbours):
                    at = place[b * neighbours + k]
                    total = total + pair(
                        *(row_of(far_pos, at * 3 + f) for f in range(3)), row_of(far_smooth, at), row_of(far_gain, at)
                    )
                total = total[0:8] + total[8:16] + total[16:24]
                near_sum = sums[b]
                grad = own * ((2.0 * KERNEL_NORM) / (h * h * h * h * h))
                kick = TIME_STEP * period.astype(F32)
                acc = []
                for f, place_f in enumerate((x, y, z)):
                    one = grad * (place_f * near_sum[0:1] - near_sum[f + 1 : f + 2])
                    two = place_f * total[0:1] - total[f + 1 : f + 2]
                    acc.append(one + two)
                heat = (
                    (x * u + y * v + z * w) * near_sum[0:1]
                    - (u * near_sum[1:2] + v * near_sum[2:3] + w * near_sum[3:4])
                    - (x * near_sum[4:5] + y * near_sum[5:6] + z * near_sum[6:7])
                    + near_sum[7:8]
                )
                new_energy[pl.ds(b, 1), :] = row_of(energy, b) - kick * (grad * heat)
                for f, (speed, place_f) in enumerate(((u, x), (v, y), (w, z))):
                    now = speed + kick * acc[f]
                    new_vel[b, f : f + 1, :] = now
                    new_pos[b, f : f + 1, :] = place_f + TIME_STEP * now

            @pl.when(jnp.logical_not(active))
            def _():
                new_energy[pl.ds(b, 1), :] = row_of(energy, b)
                new_vel[b] = vel[b]
                new_pos[b] = pos[b] + TIME_STEP * vel[b]

            return 0

        lax.fori_loop(0, pos.shape[0], block, 0)
        send_rows(pick, send_pos, lambda slot, f: new_pos[slot, f : f + 1, :], 3)

    return body


def gas_sides(pos, sides):
    def one(b, _):
        x, y, z = (pos[b, f : f + 1, :] for f in range(3))
        sides[b] = near_side(rows8(-2.0 * x, -2.0 * y, -2.0 * z, 1.0, norm_sq(x, y, z)))
        return 0

    blocks = pos.shape[0]
    lax.fori_loop(0, blocks, one, 0)
    sides[blocks] = jnp.zeros(sides.shape[1:], BF16)


def omega_of(star, c, when, sides, widths, slot):
    x, y, z = (star[c, f : f + 1, :] + when * star[c, f + 3 : f + 4, :] for f in range(3))
    far = far_side(rows8(x, y, z, norm_sq(x, y, z), 1.0))
    dist_sq = jnp.maximum(outer(sides[slot], far), 1e-30)
    wide = dist_sq + widths[slot]
    return (1.0 - dist_sq * lax.rsqrt(dist_sq * wide)) * jnp.exp2(dist_sq * star[c, 6:7, :])


def omega_kernel(substep):
    when = (substep + 1) * TIME_STEP

    def body(list_c, list_slot, list_out, number, pos, widths, star, part, sides, room):
        gas_sides(pos, sides)
        room[...] = jnp.zeros_like(room)

        def group(at, _):
            for lane in range(UNROLL):
                e = at * UNROLL + lane
                omega = omega_of(star, list_c[e], when, sides, widths, list_slot[e])
                room[pl.ds(list_out[e], 1), :] = jnp.sum(omega, axis=0, keepdims=True)
            return 0

        lax.fori_loop(0, number[0], group, 0)
        part[...] = room[0 : part.shape[0], :]

    return body


def deposit_kernel(substep, last):
    when = (substep + 1) * TIME_STEP

    def body(
        list_c, list_slot, number, pick, pos, widths, star, pay, total, mass, vel, energy, metals, density, *rest
    ):
        if last:
            new_mass, new_vel, new_energy, new_metals, sides, dep = rest
        else:
            new_mass, new_vel, new_energy, new_metals, send_mass, send_vel, sides, dep = rest
        gas_sides(pos, sides)
        dep[...] = jnp.zeros_like(dep)

        def group(at, _):
            parts = []
            for lane in range(UNROLL):
                e = at * UNROLL + lane
                c, slot = list_c[e], list_slot[e]
                omega = two_halves(omega_of(star, c, when, sides, widths, slot))
                load = pay[c] * (1.0 / row_of(total, c))
                first = load.astype(BF16).astype(F32)
                left = jnp.concatenate([first, load - first], axis=0).astype(BF16)
                out = inner(jnp.concatenate([left, left], axis=1), omega)
                parts.append((slot, out[0:24] + out[24:48]))
            for slot, out in parts:
                dep[slot] = dep[slot] + out
            return 0

        lax.fori_loop(0, number[0], group, 0)

        def block(b, _):
            got = dep[b]
            m = row_of(mass, b)
            grown = m + got[0:1]
            new_mass[pl.ds(b, 1), :] = grown
            new_vel[b] = (m * vel[b] + got[1:4]) / grown
            cooled = ENERGY_FLOOR + (row_of(energy, b) - ENERGY_FLOOR) * jnp.exp(
                (-TIME_STEP * COOL_RATE) * row_of(density, b)
            )
            new_energy[pl.ds(b, 1), :] = (m * cooled + got[4:5]) / grown
            new_metals[b] = metals[b] + got[8:24]
            return 0

        lax.fori_loop(0, pos.shape[0], block, 0)
        if not last:
            send_rows(pick, send_mass, lambda slot, f: row_of(new_mass, slot), 1)
            send_rows(pick, send_vel, lambda slot, f: new_vel[slot, f : f + 1, :], 3)

    return body


def local(
    gas_pos, gas_vel, gas_mass, gas_smooth, gas_energy, gas_metals, gas_bins, gas_nbr_dev, gas_nbr_slot,
    star_pos, star_vel, star_radius, star_mdot, star_edot, star_yields, star_ovl_dev, star_ovl_slot,
):
    peers = lax.axis_size(AXES)
    nb, neighbours = gas_nbr_dev.shape
    sb, entries = star_ovl_dev.shape
    width = gas_pos.shape[2]
    loads = 24
    cap = max(2, 2 * nb * neighbours // peers)
    span = cap + sb
    stars = peers * sb
    sent = peers * cap
    i32 = jnp.int32

    with jax.named_scope("star_data"):
        ejecta = star_mdot * TIME_STEP
        reach = -LOG2E / (star_radius * star_radius)
        star8 = jnp.concatenate([star_pos, star_vel, reach[:, None], jnp.zeros_like(reach)[:, None]], axis=1)
        pay = jnp.concatenate(
            [
                ejecta[:, None],
                ejecta[:, None] * star_vel,
                (star_edot * TIME_STEP)[:, None],
                jnp.zeros((sb, 3, width), F32),
                ejecta[:, None] * star_yields,
            ],
            axis=1,
        )
        widths = jnp.broadcast_to((gas_smooth * gas_smooth)[:, :, None], (nb, width, width))
        widths = jnp.concatenate([widths, jnp.ones((1, width, width), F32)], axis=0)

    with jax.named_scope("plan"):
        req, place = call(
            plan_kernel(peers, cap, sb, neighbours, entries),
            [((peers * span,), i32), ((nb * neighbours,), i32)],
            [SMEM] * 4,
            [pltpu.SMEM((peers,), i32)],
            smem_outs=(0, 1),
        )(gas_nbr_dev.reshape(-1), gas_nbr_slot.reshape(-1), star_ovl_dev.reshape(-1), star_ovl_slot.reshape(-1))
        asked = swap(req.reshape(peers, span)).reshape(-1)
        pick, list_c, list_slot, list_out, number = call(
            list_kernel(peers, cap, sb, nb),
            [((sent,), i32)] + [((stars + 2 * UNROLL,), i32)] * 3 + [((1,), i32)],
            [SMEM],
            smem_outs=range(5),
        )(asked)

    with jax.named_scope("start"):
        sends = call(
            start_kernel,
            [((sent * 3, width), F32), ((sent * 3, width), F32), ((sent, width), F32), ((sent, width), F32)],
            [SMEM] + [VMEM] * 4,
        )(pick, gas_pos, gas_vel, gas_mass, gas_smooth)
        far_pos, far_vel, far_mass, far_smooth = (swap(one) for one in sends)

    with jax.named_scope("star_share"):
        all_stars = lax.all_gather(jnp.concatenate([star8, pay], axis=1), AXES, axis=0, tiled=True)
        all_star8, all_pay = all_stars[:, 0:8], all_stars[:, 8:32]

    pos, vel, mass, energy, metals = gas_pos, gas_vel, gas_mass, gas_energy, gas_metals
    sides = pltpu.VMEM((nb + 1, width, 48), BF16)
    for substep in range(SUBSTEPS):
        last = substep == SUBSTEPS - 1
        with jax.named_scope("density"):
            sums, term, gain, density, send_gain = call(
                density_kernel(neighbours),
                [((nb, 8, width), F32)] + [((nb, width), F32)] * 3 + [((sent, width), F32)],
                [SMEM] * 2 + [VMEM] * 8,
            )(place, pick, pos, vel, mass, gas_smooth, energy, far_pos, far_vel, far_mass)
            far_gain = swap(send_gain)
        with jax.named_scope("force"):
            pos, vel, energy, send_pos = call(
                force_kernel(neighbours, substep),
                [((nb, 3, width), F32), ((nb, 3, width), F32), ((nb, width), F32), ((sent * 3, width), F32)],
                [SMEM] * 3 + [VMEM] * 10,
            )(place, pick, gas_bins, pos, vel, gas_smooth, energy, term, gain, sums, far_pos, far_smooth, far_gain)
            if not last:
                far_pos = swap(send_pos)
        with jax.named_scope("omega"):
            part = call(
                omega_kernel(substep),
                [((stars, width), F32)],
                [SMEM] * 4 + [VMEM] * 3,
                [sides, pltpu.VMEM((stars + 8, width), F32)],
            )(list_c, list_slot, list_out, number, pos, widths, all_star8)[0]
            totals = jnp.sum(swap(part).reshape(peers, sb, width), axis=0)
            total = swap(jnp.broadcast_to(totals[None], (peers, sb, width)).reshape(stars, width))
        with jax.named_scope("deposit"):
            outs = call(
                deposit_kernel(substep, last),
                [((nb, width), F32), ((nb, 3, width), F32), ((nb, width), F32), ((nb, 16, width), F32)]
                + ([] if last else [((sent, width), F32), ((sent * 3, width), F32)]),
                [SMEM] * 4 + [VMEM] * 10,
                [sides, pltpu.VMEM((nb + 1, loads, width), F32)],
            )(
                list_c, list_slot, number, pick, pos, widths, all_star8, all_pay, total,
                mass, vel, energy, metals, density,
            )
            mass, vel, energy, metals = outs[:4]
            if not last:
                far_mass, far_vel = swap(outs[4]), swap(outs[5])
    return (pos, vel, mass, energy, metals)


def solution(mesh):
    split = [P(AXES, *([None] * (rank - 1))) for rank in (3, 3, 2, 2, 2, 3, 1, 2, 2, 3, 3, 2, 2, 2, 3, 2, 2)]
    return jax.shard_map(
        local,
        mesh=mesh,
        in_specs=tuple(split),
        out_specs=tuple(P(AXES, *([None] * (rank - 1))) for rank in (3, 3, 2, 2, 3)),
        check_vma=False,
    )
```

```python
import jax
import jax.numpy as jnp
from jax import lax
from jax.experimental import pallas as pl
from jax.experimental.pallas import tpu as pltpu
from jax.sharding import PartitionSpec as P

SUBSTEPS = 4
KERNEL_NORM = 0.1795871221251666
GAMMA_LESS = 0.6666666666666666
TIME_STEP = 0.05
COOL_RATE = 0.4
ENERGY_FLOOR = 0.2
LOG2E = 1.4426950408889634
AXES = ("gx", "gy")
F32 = jnp.float32
BF16 = jnp.bfloat16
GROUP = 4
WIDE = 16
TEAM = 4
VMEM = pl.BlockSpec(memory_space=pltpu.VMEM)
SMEM = pl.BlockSpec(memory_space=pltpu.SMEM)
PARAMS = pltpu.CompilerParams(vmem_limit_bytes=48 * 1024 * 1024)


def call(body, outs, ins, scratch=(), smem_outs=(), work=0):
    return pl.pallas_call(
        body,
        out_shape=[jax.ShapeDtypeStruct(shape, dtype) for shape, dtype in outs],
        in_specs=ins,
        out_specs=[SMEM if at in smem_outs else VMEM for at in range(len(outs))],
        scratch_shapes=list(scratch),
        compiler_params=PARAMS,
        cost_estimate=pl.CostEstimate(flops=work, bytes_accessed=0, transcendentals=0) if work else None,
    )


def swap(payload):
    return lax.all_to_all(payload, AXES, split_axis=0, concat_axis=0, tiled=True)


def row_of(ref, at):
    return ref[pl.ds(at, 1), :]


def rows8(*rows):
    place = lax.broadcasted_iota(jnp.int32, (8, 128), 0)
    out = jnp.zeros((8, 128), F32)
    for at, row in enumerate(rows):
        out = jnp.where(place == at, row, out)
    return out


def split3(value):
    first = value.astype(BF16).astype(F32)
    rest = value - first
    second = rest.astype(BF16).astype(F32)
    third = (rest - second).astype(BF16).astype(F32)
    return first, second, third


def far_side(value):
    a, b, c = split3(value)
    return jnp.concatenate([a, a, b, b, a, c], axis=0).astype(BF16)


def near_side(value):
    a, b, c = split3(value)
    return jnp.concatenate([a, b, a, b, c, a], axis=0).T.astype(BF16)


def weights(value):
    a, b, c = split3(value)
    packed = jnp.concatenate([a, b, c, jnp.zeros_like(a)], axis=0).astype(BF16)
    return jnp.concatenate([packed, packed], axis=1)


def two_halves(value):
    first = value.astype(BF16)
    second = (value - first.astype(F32)).astype(BF16)
    return jnp.concatenate([first, second], axis=1)


def inner(left, right):
    return lax.dot_general(left, right, (((1,), (1,)), ((), ())), preferred_element_type=F32)


def outer(left, right):
    return lax.dot_general(left, right, (((1,), (0,)), ((), ())), preferred_element_type=F32)


def norm_sq(x, y, z):
    return x * x + y * y + z * z


def plan_kernel(peers, cap, sb):
    span = cap + sb

    def body(gas_dev, gas_slot, star_dev, star_slot, req, place, count):
        rows, neighbours = gas_dev.shape
        entries = star_dev.shape[1]

        def clear(d, _):
            count[d] = 0
            for c in range(span):
                req[d * span + c] = -1
            return 0

        def gas(b, _):
            for k in range(neighbours):
                dev = gas_dev[b, k]
                used = count[dev]
                count[dev] = used + 1
                req[dev * span + used] = gas_slot[b, k]
                place[b * neighbours + k] = dev * cap + used
            return 0

        def star(c, _):
            for at in range(entries):
                req[star_dev[c, at] * span + cap + c] = star_slot[c, at]
            return 0

        lax.fori_loop(0, peers, clear, 0)
        lax.fori_loop(0, rows, gas, 0)
        lax.fori_loop(0, sb, star, 0)

    return body


def list_sizes(stars, nb):
    room = stars + nb * GROUP + WIDE
    room = -(-room // WIDE) * WIDE
    return room, room + stars


def list_kernel(peers, cap, sb, nb):
    span = cap + sb
    room, whole = list_sizes(peers * sb, nb)

    def body(asked, list_c, list_slot, number, count):
        for b in range(nb + 1):
            count[b] = 0

        def clear(at, _):
            for g in range(GROUP):
                list_c[at * GROUP + g] = -1
            list_slot[at] = nb
            return 0

        lax.fori_loop(0, room // GROUP, clear, 0, unroll=2)

        def tally(d, _):
            for c in range(sb):
                slot = asked[d * span + cap + c] + 1
                count[slot] = count[slot] + 1
            return 0

        lax.fori_loop(0, peers, tally, 0)
        count[0] = room
        used = 0
        for b in range(nb):
            more = (count[b + 1] + GROUP - 1) // GROUP * GROUP
            count[b + 1] = used
            used = used + more
        number[0] = (used + WIDE - 1) // WIDE

        def deal(d, _):
            for c in range(sb):
                slot = asked[d * span + cap + c]
                at = count[slot + 1]
                count[slot + 1] = at + 1
                list_c[at] = d * sb + c
                list_slot[at // GROUP] = slot
            return 0

        lax.fori_loop(0, peers, deal, 0)

    return body


def send_rows(asked, out, source, width, cap, span):
    def one(d, _):
        for c in range(cap):
            slot = jnp.maximum(asked[d * span + c], 0)
            for f in range(width):
                out[pl.ds((d * cap + c) * width + f, 1), :] = source(slot, f)
        return 0

    lax.fori_loop(0, out.shape[0] // (cap * width), one, 0)


def start_kernel(cap, span):
    def body(asked, pos, vel, mass, smooth, send, widths):
        def source(slot, f):
            if f < 3:
                return pos[slot, f : f + 1, :]
            if f >= 5:
                return vel[slot, f - 5 : f - 4, :]
            return row_of(smooth if f == 3 else mass, slot)

        send_rows(asked, send, source, 8, cap, span)
        blocks = pos.shape[0]

        def one(b, _):
            h = row_of(smooth, b)
            widths[b] = jnp.broadcast_to(h * h, widths.shape[1:]).T
            return 0

        lax.fori_loop(0, blocks, one, 0, unroll=2)
        widths[blocks] = jnp.ones(widths.shape[1:], F32)

    return body


def share_kernel(star_pos, star_vel, star_radius, star_mdot, star_edot, star_yields, share):
    for c in range(star_pos.shape[0]):
        radius = star_radius[c : c + 1, :]
        ejecta = star_mdot[c : c + 1, :] * TIME_STEP
        share[c, 0:3, :] = star_pos[c]
        share[c, 3:6, :] = star_vel[c]
        share[c, 6:7, :] = -LOG2E / (radius * radius)
        share[c, 7:8, :] = jnp.zeros_like(ejecta)
        share[c, 8:9, :] = ejecta
        share[c, 9:12, :] = ejecta * star_vel[c]
        share[c, 12:13, :] = star_edot[c : c + 1, :] * TIME_STEP
        share[c, 13:16, :] = jnp.zeros_like(star_vel[c])
        share[c, 16:32, :] = ejecta * star_yields[c]


def total_kernel(peers):
    def body(parts, total):
        sb = total.shape[0] // peers
        now = parts[0:sb, :]
        for d in range(1, peers):
            now = now + parts[d * sb : (d + 1) * sb, :]
        for d in range(peers):
            total[d * sb : (d + 1) * sb, :] = now

    return body


def team_sums(jobs):
    exponents = [[outer(near, far) for near, far, _ in team] for team in jobs]
    reaches = [[two_halves(jnp.exp2(one)) for one in team] for team in exponents]
    results = []
    for team, parts in zip(jobs, reaches):
        total = None
        for (_, _, load), part in zip(team, parts):
            one = inner(part, load)
            total = one if total is None else total + one
        total = total.T
        results.append(total[0:8] + total[8:16] + total[16:24])
    return results


def density_kernel(neighbours, cap, span, first):
    def body(asked, place, pos, vel, mass, smooth, energy, *rest):
        if first:
            far0, sums, term, gain, density, send_gain = rest
        else:
            far_pos, far_mv, sums, term, gain, density, send_gain = rest

        def ghost(at):
            if first:
                return [row_of(far0, at * 8 + f) for f in (0, 1, 2, 5, 6, 7, 4)]
            return [row_of(far_pos, at * 3 + f) for f in range(3)] + [row_of(far_mv, at * 4 + f) for f in (1, 2, 3, 0)]

        def pair(near, px, py, pz, vx, vy, vz, m):
            far = far_side(rows8(px, py, pz, norm_sq(px, py, pz), 1.0))
            load = rows8(m, m * px, m * py, m * pz, m * vx, m * vy, m * vz, m * (px * vx + py * vy + pz * vz))
            return near, far, weights(load)

        def team(at, _):
            jobs = []
            for g in range(TEAM):
                b = at * TEAM + g
                x, y, z = (pos[b, f : f + 1, :] for f in range(3))
                h = row_of(smooth, b)
                scale = LOG2E / (h * h)
                near = near_side(
                    rows8(2.0 * scale * x, 2.0 * scale * y, 2.0 * scale * z, -scale, -scale * norm_sq(x, y, z))
                )
                own = [pair(near, x, y, z, *(vel[b, f : f + 1, :] for f in range(3)), row_of(mass, b))]
                jobs.append(own + [pair(near, *ghost(place[b * neighbours + k])) for k in range(neighbours)])
            for g, total in enumerate(team_sums(jobs)):
                b = at * TEAM + g
                h = row_of(smooth, b)
                sums[b] = total
                dense = KERNEL_NORM * total[0:1] / (h * h * h)
                density[pl.ds(b, 1), :] = dense
                own = GAMMA_LESS * row_of(energy, b) / dense
                term[pl.ds(b, 1), :] = own
                gain[pl.ds(b, 1), :] = row_of(mass, b) * own * ((2.0 * KERNEL_NORM) / (h * h * h * h * h))
            return 0

        lax.fori_loop(0, pos.shape[0] // TEAM, team, 0)
        send_rows(asked, send_gain, lambda slot, f: row_of(gain, slot), 1, cap, span)

    return body


def force_kernel(neighbours, cap, span, substep, first, last):
    def body(asked, place, bins, pos, vel, smooth, energy, term, gain, sums, far0, *rest):
        if first:
            far_gain, new_pos, new_vel, new_energy = rest[:4]
        else:
            far_pos, far_gain, new_pos, new_vel, new_energy = rest[:5]
        busy = rest[-1]

        def ghost(at):
            if first:
                return [row_of(far0, at * 8 + f) for f in range(4)] + [row_of(far_gain, at)]
            return [row_of(far_pos, at * 3 + f) for f in range(3)] + [row_of(far0, at * 8 + 3), row_of(far_gain, at)]

        def pair(near, px, py, pz, width, push):
            scale = LOG2E / (width * width)
            far = far_side(rows8(scale * px, scale * py, scale * pz, scale * norm_sq(px, py, pz), scale))
            return near, far, weights(rows8(push, push * px, push * py, push * pz))

        new_energy[...] = energy[...]
        used = 0
        for b in range(pos.shape[0]):
            new_vel[b] = vel[b]
            new_pos[b] = pos[b] + TIME_STEP * vel[b]
            period = jnp.left_shift(1, bins[b])
            busy[used] = b
            used = used + jnp.where((substep & (period - 1)) == 0, 1, 0)
        edge = busy[jnp.maximum(used - 1, 0)]
        for extra in range(TEAM):
            busy[used + extra] = edge

        def team(at, _):
            jobs = []
            for g in range(TEAM):
                b = busy[at * TEAM + g]
                x, y, z = (pos[b, f : f + 1, :] for f in range(3))
                near = near_side(rows8(2.0 * x, 2.0 * y, 2.0 * z, -1.0, -norm_sq(x, y, z)))
                own = [pair(near, x, y, z, row_of(smooth, b), row_of(gain, b))]
                jobs.append(own + [pair(near, *ghost(place[b * neighbours + k])) for k in range(neighbours)])
            for g, total in enumerate(team_sums(jobs)):
                b = busy[at * TEAM + g]
                x, y, z = (pos[b, f : f + 1, :] for f in range(3))
                u, v, w = (vel[b, f : f + 1, :] for f in range(3))
                h = row_of(smooth, b)
                near_sum = sums[b]
                grad = row_of(term, b) * ((2.0 * KERNEL_NORM) / (h * h * h * h * h))
                kick = TIME_STEP * jnp.left_shift(1, bins[b]).astype(F32)
                heat = (
                    (x * u + y * v + z * w) * near_sum[0:1]
                    - (u * near_sum[1:2] + v * near_sum[2:3] + w * near_sum[3:4])
                    - (x * near_sum[4:5] + y * near_sum[5:6] + z * near_sum[6:7])
                    + near_sum[7:8]
                )
                new_energy[pl.ds(b, 1), :] = row_of(energy, b) - kick * (grad * heat)
                for f, (speed, spot) in enumerate(((u, x), (v, y), (w, z))):
                    one = grad * (spot * near_sum[0:1] - near_sum[f + 1 : f + 2])
                    two = spot * total[0:1] - total[f + 1 : f + 2]
                    now = speed + kick * (one + two)
                    new_vel[b, f : f + 1, :] = now
                    new_pos[b, f : f + 1, :] = spot + TIME_STEP * now
            return 0

        lax.fori_loop(0, (used + TEAM - 1) // TEAM, team, 0)
        if not last:
            send_rows(asked, rest[-2], lambda slot, f: new_pos[slot, f : f + 1, :], 3, cap, span)

    return body


def gas_sides(pos, sides):
    def one(b, _):
        x, y, z = (pos[b, f : f + 1, :] for f in range(3))
        sides[b] = near_side(rows8(-2.0 * x, -2.0 * y, -2.0 * z, 1.0, norm_sq(x, y, z)))
        return 0

    blocks = pos.shape[0]
    lax.fori_loop(0, blocks, one, 0, unroll=4)
    sides[blocks] = jnp.zeros(sides.shape[1:], BF16)


def omegas(list_c, list_slot, at, when, star, sides, widths):
    entries = []
    for e in range(WIDE):
        entries.append((list_c[at * WIDE + e], list_slot[at * (WIDE // GROUP) + e // GROUP]))
    dist = []
    for c, slot in entries:
        c = jnp.maximum(c, 0)
        x, y, z = (star[c, f : f + 1, :] + when * star[c, f + 3 : f + 4, :] for f in range(3))
        dist.append(outer(sides[slot], far_side(rows8(x, y, z, norm_sq(x, y, z), 1.0))))
    out = []
    for (c, slot), one in zip(entries, dist):
        one = jnp.maximum(one, 1e-30)
        wide = one + widths[slot]
        reach = star[jnp.maximum(c, 0), 6:7, :]
        out.append((c, slot, (1.0 - one * lax.rsqrt(one * wide)) * jnp.exp2(one * reach)))
    return out


def omega_kernel(substep):
    when = (substep + 1) * TIME_STEP

    def body(list_c, list_slot, number, pos, widths, star, part, sides, room):
        gas_sides(pos, sides)
        room[...] = jnp.zeros_like(room)
        trash = part.shape[0]

        def group(at, _):
            for c, _, omega in omegas(list_c, list_slot, at, when, star, sides, widths):
                room[pl.ds(jnp.where(c < 0, trash, c), 1), :] = jnp.sum(omega, axis=0, keepdims=True)
            return 0

        lax.fori_loop(0, number[0], group, 0)
        part[...] = room[0 : part.shape[0], :]

    return body


def deposit_kernel(substep, last, cap, span):
    when = (substep + 1) * TIME_STEP

    def body(
        asked, list_c, list_slot, number, pos, widths, star, pay, total, mass, vel, energy, metals, density, *rest
    ):
        new_mass, new_vel, new_energy, new_metals = rest[:4]
        sides, dep = rest[-2:]
        gas_sides(pos, sides)
        dep[...] = jnp.zeros_like(dep)

        def group(at, _):
            found = omegas(list_c, list_slot, at, when, star, sides, widths)
            rights = [two_halves(omega) for _, _, omega in found]
            lefts = []
            for c, _, _ in found:
                flag = jnp.where(c < 0, 0.0, 1.0)
                c = jnp.maximum(c, 0)
                load = pay[c] * (flag / row_of(total, c))
                first = load.astype(BF16).astype(F32)
                left = jnp.concatenate([first, load - first], axis=0).astype(BF16)
                lefts.append(jnp.concatenate([left, left], axis=1))
            for g in range(0, WIDE, GROUP):
                out = None
                for right, left in zip(rights[g : g + GROUP], lefts[g : g + GROUP]):
                    one = inner(right, left)
                    out = one if out is None else out + one
                slot = found[g][1]
                dep[slot] = dep[slot] + out
            return 0

        lax.fori_loop(0, number[0], group, 0)

        def block(b, _):
            got = dep[b].T
            got = got[0:24] + got[24:48]
            m = row_of(mass, b)
            grown = m + got[0:1]
            new_mass[pl.ds(b, 1), :] = grown
            new_vel[b] = (m * vel[b] + got[1:4]) / grown
            cooled = ENERGY_FLOOR + (row_of(energy, b) - ENERGY_FLOOR) * jnp.exp(
                (-TIME_STEP * COOL_RATE) * row_of(density, b)
            )
            new_energy[pl.ds(b, 1), :] = (m * cooled + got[4:5]) / grown
            new_metals[b] = metals[b] + got[8:24]
            return 0

        lax.fori_loop(0, pos.shape[0], block, 0, unroll=4)
        if not last:
            send_rows(
                asked,
                rest[4],
                lambda slot, f: new_vel[slot, f - 1 : f, :] if f else row_of(new_mass, slot),
                4,
                cap,
                span,
            )

    return body


def local(
    gas_pos, gas_vel, gas_mass, gas_smooth, gas_energy, gas_metals, gas_bins, gas_nbr_dev, gas_nbr_slot,
    star_pos, star_vel, star_radius, star_mdot, star_edot, star_yields, star_ovl_dev, star_ovl_slot,
):
    peers = lax.axis_size(AXES)
    nb, neighbours = gas_nbr_dev.shape
    sb = star_ovl_dev.shape[0]
    width = gas_pos.shape[2]
    cap = max(2, 2 * nb * neighbours // peers)
    span = cap + sb
    stars = peers * sb
    sent = peers * cap
    i32 = jnp.int32
    room, whole = list_sizes(stars, nb)
    heavy = 10**10

    with jax.named_scope("plan"):
        req, place = call(
            plan_kernel(peers, cap, sb),
            [((peers * span,), i32), ((nb * neighbours,), i32)],
            [SMEM] * 4,
            [pltpu.SMEM((peers,), i32)],
            smem_outs=(0, 1),
        )(gas_nbr_dev, gas_nbr_slot, star_ovl_dev, star_ovl_slot)
        asked = swap(req.reshape(peers, span)).reshape(-1)

    with jax.named_scope("share"):
        share = call(share_kernel, [((sb, 32, width), F32)], [VMEM] * 6)(
            star_pos, star_vel, star_radius, star_mdot, star_edot, star_yields
        )[0]
        all_stars = lax.all_gather(share, AXES, axis=0, tiled=True)
        all_star8, all_pay = all_stars[:, 0:8], all_stars[:, 8:32]

    with jax.named_scope("start"):
        send0, widths = call(
            start_kernel(cap, span),
            [((sent * 8, width), F32), ((nb + 1, width, width), F32)],
            [SMEM] + [VMEM] * 4,
        )(asked, gas_pos, gas_vel, gas_mass, gas_smooth)
        far0 = swap(send0)
        list_c, list_slot, number = call(
            list_kernel(peers, cap, sb, nb),
            [((whole,), i32), ((whole // GROUP,), i32), ((1,), i32)],
            [SMEM],
            [pltpu.SMEM((nb + 1,), i32)],
            smem_outs=range(3),
        )(asked)

    pos, vel, mass, energy, metals = gas_pos, gas_vel, gas_mass, gas_energy, gas_metals
    sides = pltpu.VMEM((nb + 1, width, 48), BF16)
    block3, block1 = ((nb, 3, width), F32), ((nb, width), F32)
    for substep in range(SUBSTEPS):
        first, last = substep == 0, substep == SUBSTEPS - 1
        with jax.named_scope("density"):
            far = [far0] if first else [far_pos, far_mv]
            sums, term, gain, density, send_gain = call(
                density_kernel(neighbours, cap, span, first),
                [((nb, 8, width), F32), block1, block1, block1, ((sent, width), F32)],
                [SMEM] * 2 + [VMEM] * (5 + len(far)),
                work=heavy,
            )(asked, place, pos, vel, mass, gas_smooth, energy, *far)
            far_gain = swap(send_gain)
        with jax.named_scope("force"):
            far = [far0] if first else [far0, far_pos]
            outs = call(
                force_kernel(neighbours, cap, span, substep, first, last),
                [block3, block3, block1] + ([] if last else [((sent * 3, width), F32)]),
                [SMEM] * 3 + [VMEM] * (8 + len(far)),
                [pltpu.SMEM((nb + TEAM,), i32)],
                work=heavy,
            )(asked, place, gas_bins, pos, vel, gas_smooth, energy, term, gain, sums, *far, far_gain)
            pos, vel, energy = outs[:3]
            if not last:
                far_pos = swap(outs[3])
        with jax.named_scope("omega"):
            part = call(
                omega_kernel(substep),
                [((stars, width), F32)],
                [SMEM] * 3 + [VMEM] * 3,
                [sides, pltpu.VMEM((stars + 8, width), F32)],
                work=heavy,
            )(list_c, list_slot, number, pos, widths, all_star8)[0]
            if not last:
                part, far_pos = lax.optimization_barrier((part, far_pos))
            total = swap(call(total_kernel(peers), [((stars, width), F32)], [VMEM])(swap(part))[0])
        with jax.named_scope("deposit"):
            outs = call(
                deposit_kernel(substep, last, cap, span),
                [block1, block3, block1, ((nb, 16, width), F32)] + ([] if last else [((sent * 4, width), F32)]),
                [SMEM] * 4 + [VMEM] * 10,
                [sides, pltpu.VMEM((nb + 1, width, 48), F32)],
                work=heavy,
            )(asked, list_c, list_slot, number, pos, widths, all_star8, all_pay, total, mass, vel, energy, metals, density)
            mass, vel, energy, metals = outs[:4]
            if not last:
                far_mv = swap(outs[4])
    return (pos, vel, mass, energy, metals)


def solution(mesh):
    split = [P(AXES, *([None] * (rank - 1))) for rank in (3, 3, 2, 2, 2, 3, 1, 2, 2, 3, 3, 2, 2, 2, 3, 2, 2)]
    return jax.shard_map(
        local,
        mesh=mesh,
        in_specs=tuple(split),
        out_specs=tuple(P(AXES, *([None] * (rank - 1))) for rank in (3, 3, 2, 2, 3)),
        check_vma=False,
    )
```

```python
import jax
import jax.numpy as jnp
from jax import lax
from jax.experimental import pallas as pl
from jax.experimental.pallas import tpu as pltpu
from jax.sharding import PartitionSpec as P

SUBSTEPS = 4
KERNEL_NORM = 0.1795871221251666
GAMMA_LESS = 0.6666666666666666
TIME_STEP = 0.05
COOL_RATE = 0.4
ENERGY_FLOOR = 0.2
LOG2E = 1.4426950408889634
AXES = ("gx", "gy")
F32 = jnp.float32
BF16 = jnp.bfloat16
GROUP = 4
WIDE = 16
TEAM = 4
VMEM = pl.BlockSpec(memory_space=pltpu.VMEM)
SMEM = pl.BlockSpec(memory_space=pltpu.SMEM)
PARAMS = pltpu.CompilerParams(vmem_limit_bytes=52 * 1024 * 1024)


def call(body, outs, ins, scratch=(), smem_outs=(), work=0):
    return pl.pallas_call(
        body,
        out_shape=[jax.ShapeDtypeStruct(shape, dtype) for shape, dtype in outs],
        in_specs=ins,
        out_specs=[SMEM if at in smem_outs else VMEM for at in range(len(outs))],
        scratch_shapes=list(scratch),
        compiler_params=PARAMS,
        cost_estimate=pl.CostEstimate(flops=work, bytes_accessed=0, transcendentals=0) if work else None,
    )


def swap(payload):
    return lax.all_to_all(payload, AXES, split_axis=0, concat_axis=0, tiled=True)


def row_of(ref, at):
    return ref[pl.ds(at, 1), :]


def rows8(*rows):
    place = lax.broadcasted_iota(jnp.int32, (8, 128), 0)
    out = jnp.zeros((8, 128), F32)
    for at, row in enumerate(rows):
        out = jnp.where(place == at, row, out)
    return out


def split3(value):
    first = value.astype(BF16).astype(F32)
    rest = value - first
    second = rest.astype(BF16).astype(F32)
    third = (rest - second).astype(BF16).astype(F32)
    return first, second, third


def far_side(value):
    a, b, c = split3(value)
    return jnp.concatenate([a, a, b, b, a, c], axis=0).astype(BF16)


def near_side(value):
    a, b, c = split3(value)
    return jnp.concatenate([a, b, a, b, c, a], axis=0).T.astype(BF16)


def weights(value):
    a, b, c = split3(value)
    packed = jnp.concatenate([a, b, c, jnp.zeros_like(a)], axis=0).astype(BF16)
    return jnp.concatenate([packed, packed], axis=1)


def two_halves(value):
    first = value.astype(BF16)
    second = (value - first.astype(F32)).astype(BF16)
    return jnp.concatenate([first, second], axis=1)


def inner(left, right):
    return lax.dot_general(left, right, (((1,), (1,)), ((), ())), preferred_element_type=F32)


def outer(left, right):
    return lax.dot_general(left, right, (((1,), (0,)), ((), ())), preferred_element_type=F32)


def norm_sq(x, y, z):
    return x * x + y * y + z * z


def plan_kernel(peers, cap, sb):
    span = cap + sb

    def body(gas_dev, gas_slot, star_dev, star_slot, req, place, count):
        rows, neighbours = gas_dev.shape
        entries = star_dev.shape[1]

        def clear(d, _):
            count[d] = 0
            for c in range(span):
                req[d * span + c] = -1
            return 0

        def gas(b, _):
            for k in range(neighbours):
                dev = gas_dev[b, k]
                used = count[dev]
                count[dev] = used + 1
                req[dev * span + used] = gas_slot[b, k]
                place[b * neighbours + k] = dev * cap + used
            return 0

        def star(c, _):
            for at in range(entries):
                req[star_dev[c, at] * span + cap + c] = star_slot[c, at]
            return 0

        lax.fori_loop(0, peers, clear, 0)
        lax.fori_loop(0, rows, gas, 0)
        lax.fori_loop(0, sb, star, 0)

    return body


def list_sizes(hits, stars, nb):
    room = -(-(hits + nb * (GROUP - 1)) // WIDE) * WIDE
    return room, room + stars


def list_kernel(peers, cap, sb, nb, hits):
    span = cap + sb
    room, whole = list_sizes(hits, peers * sb, nb)

    def body(asked, list_c, list_slot, number, count):
        for b in range(nb + 1):
            count[b] = 0

        def clear(at, _):
            for g in range(GROUP):
                list_c[at * GROUP + g] = -1
            list_slot[at] = nb
            return 0

        lax.fori_loop(0, room // GROUP, clear, 0, unroll=2)

        def tally(d, _):
            for c in range(sb):
                slot = asked[d * span + cap + c] + 1
                count[slot] = count[slot] + 1
            return 0

        lax.fori_loop(0, peers, tally, 0)
        count[0] = room
        used = 0
        for b in range(nb):
            more = (count[b + 1] + GROUP - 1) // GROUP * GROUP
            count[b + 1] = used
            used = used + more
        number[0] = (used + WIDE - 1) // WIDE

        def deal(d, _):
            for c in range(sb):
                slot = asked[d * span + cap + c]
                at = count[slot + 1]
                count[slot + 1] = at + 1
                list_c[at] = d * sb + c
                list_slot[at // GROUP] = slot
            return 0

        lax.fori_loop(0, peers, deal, 0)

    return body


def send_rows(asked, out, source, cap, span):
    width = source.shape[1]

    def one(d, _):
        base = pl.multiple_of(d * (cap * width), cap * width)
        for c in range(cap):
            slot = jnp.maximum(asked[d * span + c], 0)
            out[pl.ds(base + c * width, width), :] = source[slot]
        return 0

    lax.fori_loop(0, out.shape[0] // (cap * width), one, 0)


def start_kernel(cap, span):
    def body(asked, pos, vel, mass, smooth, send, widths, state):
        blocks = pos.shape[0]
        for b in range(blocks):
            h = smooth[b : b + 1, :]
            state[b, 0:3, :] = pos[b]
            state[b, 3:4, :] = h
            state[b, 4:5, :] = mass[b : b + 1, :]
            state[b, 5:8, :] = vel[b]
        send_rows(asked, send, state, cap, span)

        def one(b, _):
            h = row_of(smooth, b)
            widths[b] = jnp.broadcast_to(h * h, widths.shape[1:]).T
            return 0

        lax.fori_loop(0, blocks, one, 0, unroll=2)
        widths[blocks] = jnp.ones(widths.shape[1:], F32)

    return body


def share_kernel(star_pos, star_vel, star_radius, star_mdot, star_edot, star_yields, share):
    for c in range(star_pos.shape[0]):
        radius = star_radius[c : c + 1, :]
        ejecta = star_mdot[c : c + 1, :] * TIME_STEP
        share[c, 0:3, :] = star_pos[c]
        share[c, 3:6, :] = star_vel[c]
        share[c, 6:7, :] = -LOG2E / (radius * radius)
        share[c, 7:8, :] = jnp.zeros_like(ejecta)
        share[c, 8:9, :] = ejecta
        share[c, 9:12, :] = ejecta * star_vel[c]
        share[c, 12:13, :] = star_edot[c : c + 1, :] * TIME_STEP
        share[c, 13:16, :] = jnp.zeros_like(star_vel[c])
        share[c, 16:32, :] = ejecta * star_yields[c]


def total_kernel(peers):
    def body(parts, total):
        sb = total.shape[0] // peers
        now = parts[0:sb, :]
        for d in range(1, peers):
            now = now + parts[d * sb : (d + 1) * sb, :]
        for d in range(peers):
            total[d * sb : (d + 1) * sb, :] = now

    return body


def team_sums(jobs):
    exponents = [[outer(near, far) for near, far, _ in team] for team in jobs]
    reaches = [[two_halves(jnp.exp2(one)) for one in team] for team in exponents]
    results = []
    for team, parts in zip(jobs, reaches):
        total = None
        for (_, _, load), part in zip(team, parts):
            one = inner(part, load)
            total = one if total is None else total + one
        total = total.T
        results.append(total[0:8] + total[8:16] + total[16:24])
    return results


def density_kernel(neighbours, cap, span, first):
    def body(asked, place, pos, vel, mass, smooth, energy, *rest):
        if first:
            far0, sums, term, gain, density, send_gain, out_gain = rest
        else:
            far_pos, far_mv, sums, term, gain, density, send_gain, out_gain = rest

        def ghost(at):
            if first:
                return [row_of(far0, at * 8 + f) for f in (0, 1, 2, 5, 6, 7, 4)]
            return [row_of(far_pos, at * 3 + f) for f in range(3)] + [row_of(far_mv, at * 4 + f) for f in (1, 2, 3, 0)]

        def pair(near, px, py, pz, vx, vy, vz, m):
            far = far_side(rows8(px, py, pz, norm_sq(px, py, pz), 1.0))
            load = rows8(m, m * px, m * py, m * pz, m * vx, m * vy, m * vz, m * (px * vx + py * vy + pz * vz))
            return near, far, weights(load)

        def team(at, _):
            jobs = []
            for g in range(TEAM):
                b = at * TEAM + g
                x, y, z = (pos[b, f : f + 1, :] for f in range(3))
                h = row_of(smooth, b)
                scale = LOG2E / (h * h)
                near = near_side(
                    rows8(2.0 * scale * x, 2.0 * scale * y, 2.0 * scale * z, -scale, -scale * norm_sq(x, y, z))
                )
                own = [pair(near, x, y, z, *(vel[b, f : f + 1, :] for f in range(3)), row_of(mass, b))]
                jobs.append(own + [pair(near, *ghost(place[b * neighbours + k])) for k in range(neighbours)])
            for g, total in enumerate(team_sums(jobs)):
                b = at * TEAM + g
                h = row_of(smooth, b)
                sums[b] = total
                dense = KERNEL_NORM * total[0:1] / (h * h * h)
                density[pl.ds(b, 1), :] = dense
                own = GAMMA_LESS * row_of(energy, b) / dense
                term[pl.ds(b, 1), :] = own
                push = row_of(mass, b) * own * ((2.0 * KERNEL_NORM) / (h * h * h * h * h))
                gain[pl.ds(b, 1), :] = push
                out_gain[b] = push
            return 0

        lax.fori_loop(0, pos.shape[0] // TEAM, team, 0)
        send_rows(asked, send_gain, out_gain, cap, span)

    return body


def gas_sides(pos, sides):
    def one(b, _):
        x, y, z = (pos[b, f : f + 1, :] for f in range(3))
        sides[b] = near_side(rows8(-2.0 * x, -2.0 * y, -2.0 * z, 1.0, norm_sq(x, y, z)))
        return 0

    blocks = pos.shape[0]
    lax.fori_loop(0, blocks, one, 0, unroll=4)
    sides[blocks] = jnp.zeros(sides.shape[1:], BF16)


def force_kernel(neighbours, cap, span, substep, first, last):
    def body(asked, place, bins, pos, vel, smooth, energy, term, gain, sums, far0, *rest):
        if first:
            far_gain, new_pos, new_vel, new_energy = rest[:4]
        else:
            far_pos, far_gain, new_pos, new_vel, new_energy = rest[:5]
        busy = rest[-1]

        def ghost(at):
            if first:
                return [row_of(far0, at * 8 + f) for f in range(4)] + [row_of(far_gain, at)]
            return [row_of(far_pos, at * 3 + f) for f in range(3)] + [row_of(far0, at * 8 + 3), row_of(far_gain, at)]

        def pair(near, px, py, pz, width, push):
            scale = LOG2E / (width * width)
            far = far_side(rows8(scale * px, scale * py, scale * pz, scale * norm_sq(px, py, pz), scale))
            return near, far, weights(rows8(push, push * px, push * py, push * pz))

        new_energy[...] = energy[...]
        used = 0
        for b in range(pos.shape[0]):
            new_vel[b] = vel[b]
            new_pos[b] = pos[b] + TIME_STEP * vel[b]
            period = jnp.left_shift(1, bins[b])
            busy[used] = b
            used = used + jnp.where((substep & (period - 1)) == 0, 1, 0)
        edge = busy[jnp.maximum(used - 1, 0)]
        for extra in range(TEAM):
            busy[used + extra] = edge

        def team(at, _):
            jobs = []
            for g in range(TEAM):
                b = busy[at * TEAM + g]
                x, y, z = (pos[b, f : f + 1, :] for f in range(3))
                near = near_side(rows8(2.0 * x, 2.0 * y, 2.0 * z, -1.0, -norm_sq(x, y, z)))
                own = [pair(near, x, y, z, row_of(smooth, b), row_of(gain, b))]
                jobs.append(own + [pair(near, *ghost(place[b * neighbours + k])) for k in range(neighbours)])
            for g, total in enumerate(team_sums(jobs)):
                b = busy[at * TEAM + g]
                x, y, z = (pos[b, f : f + 1, :] for f in range(3))
                u, v, w = (vel[b, f : f + 1, :] for f in range(3))
                h = row_of(smooth, b)
                near_sum = sums[b]
                grad = row_of(term, b) * ((2.0 * KERNEL_NORM) / (h * h * h * h * h))
                kick = TIME_STEP * jnp.left_shift(1, bins[b]).astype(F32)
                heat = (
                    (x * u + y * v + z * w) * near_sum[0:1]
                    - (u * near_sum[1:2] + v * near_sum[2:3] + w * near_sum[3:4])
                    - (x * near_sum[4:5] + y * near_sum[5:6] + z * near_sum[6:7])
                    + near_sum[7:8]
                )
                new_energy[pl.ds(b, 1), :] = row_of(energy, b) - kick * (grad * heat)
                for f, (speed, spot) in enumerate(((u, x), (v, y), (w, z))):
                    one = grad * (spot * near_sum[0:1] - near_sum[f + 1 : f + 2])
                    two = spot * total[0:1] - total[f + 1 : f + 2]
                    now = speed + kick * (one + two)
                    new_vel[b, f : f + 1, :] = now
                    new_pos[b, f : f + 1, :] = spot + TIME_STEP * now
            return 0

        lax.fori_loop(0, (used + TEAM - 1) // TEAM, team, 0)
        gas_sides(new_pos, rest[-2])
        if not last:
            send_rows(asked, rest[-3], new_pos, cap, span)

    return body


def omegas(list_c, list_slot, at, when, star, sides, widths):
    entries = []
    for e in range(WIDE):
        entries.append((list_c[at * WIDE + e], list_slot[at * (WIDE // GROUP) + e // GROUP]))
    dist = []
    for c, slot in entries:
        c = jnp.maximum(c, 0)
        x, y, z = (star[c, f : f + 1, :] + when * star[c, f + 3 : f + 4, :] for f in range(3))
        dist.append(outer(sides[slot], far_side(rows8(x, y, z, norm_sq(x, y, z), 1.0))))
    out = []
    for (c, slot), one in zip(entries, dist):
        one = jnp.maximum(one, 1e-30)
        wide = one + widths[slot]
        reach = star[jnp.maximum(c, 0), 6:7, :]
        out.append((c, slot, (1.0 - one * lax.rsqrt(one * wide)) * jnp.exp2(one * reach)))
    return out


def omega_kernel(substep):
    when = (substep + 1) * TIME_STEP

    def body(list_c, list_slot, number, sides, widths, star, part, room):
        room[...] = jnp.zeros_like(room)
        trash = part.shape[0]

        def group(at, _):
            for c, _, omega in omegas(list_c, list_slot, at, when, star, sides, widths):
                room[pl.ds(jnp.where(c < 0, trash, c), 1), :] = jnp.sum(omega, axis=0, keepdims=True)
            return 0

        lax.fori_loop(0, number[0], group, 0)
        part[...] = room[0 : part.shape[0], :]

    return body


def deposit_kernel(substep, last, cap, span):
    when = (substep + 1) * TIME_STEP

    def body(
        asked, list_c, list_slot, number, sides, widths, star, pay, total, mass, vel, energy, metals, density, *rest
    ):
        new_mass, new_vel, new_energy, new_metals = rest[:4]
        dep = rest[-2]
        dep[...] = jnp.zeros_like(dep)

        def group(at, _):
            found = omegas(list_c, list_slot, at, when, star, sides, widths)
            rights = [two_halves(omega) for _, _, omega in found]
            lefts = []
            for c, _, _ in found:
                flag = jnp.where(c < 0, 0.0, 1.0)
                c = jnp.maximum(c, 0)
                load = pay[c] * (flag / row_of(total, c))
                first = load.astype(BF16).astype(F32)
                left = jnp.concatenate([first, load - first], axis=0).astype(BF16)
                lefts.append(jnp.concatenate([left, left], axis=1))
            for g in range(0, WIDE, GROUP):
                out = None
                for right, left in zip(rights[g : g + GROUP], lefts[g : g + GROUP]):
                    one = inner(right, left)
                    out = one if out is None else out + one
                slot = found[g][1]
                dep[slot] = dep[slot] + out
            return 0

        lax.fori_loop(0, number[0], group, 0)

        def block(b, _):
            got = dep[b].T
            got = got[0:24] + got[24:48]
            m = row_of(mass, b)
            grown = m + got[0:1]
            new_mass[pl.ds(b, 1), :] = grown
            speed = (m * vel[b] + got[1:4]) / grown
            new_vel[b] = speed
            if not last:
                state = rest[-1]
                state[b, 0:1, :] = grown
                state[b, 1:4, :] = speed
            cooled = ENERGY_FLOOR + (row_of(energy, b) - ENERGY_FLOOR) * jnp.exp(
                (-TIME_STEP * COOL_RATE) * row_of(density, b)
            )
            new_energy[pl.ds(b, 1), :] = (m * cooled + got[4:5]) / grown
            new_metals[b] = metals[b] + got[8:24]
            return 0

        lax.fori_loop(0, mass.shape[0], block, 0, unroll=4)
        if not last:
            send_rows(asked, rest[4], rest[-1], cap, span)

    return body


def local(
    gas_pos, gas_vel, gas_mass, gas_smooth, gas_energy, gas_metals, gas_bins, gas_nbr_dev, gas_nbr_slot,
    star_pos, star_vel, star_radius, star_mdot, star_edot, star_yields, star_ovl_dev, star_ovl_slot,
):
    peers = lax.axis_size(AXES)
    nb, neighbours = gas_nbr_dev.shape
    sb = star_ovl_dev.shape[0]
    width = gas_pos.shape[2]
    cap = max(2, 2 * nb * neighbours // peers)
    span = cap + sb
    stars = peers * sb
    sent = peers * cap
    i32 = jnp.int32
    hits = peers * max(2, 2 * sb * star_ovl_dev.shape[1] // peers)
    room, whole = list_sizes(hits, stars, nb)
    heavy = 10**10

    with jax.named_scope("plan"):
        req, place = call(
            plan_kernel(peers, cap, sb),
            [((peers * span,), i32), ((nb * neighbours,), i32)],
            [SMEM] * 4,
            [pltpu.SMEM((peers,), i32)],
            smem_outs=(0, 1),
        )(gas_nbr_dev, gas_nbr_slot, star_ovl_dev, star_ovl_slot)
        asked = swap(req.reshape(peers, span)).reshape(-1)

    with jax.named_scope("share"):
        req, star_pos, star_vel, star_yields = lax.optimization_barrier((req, star_pos, star_vel, star_yields))
        share = call(share_kernel, [((sb, 32, width), F32)], [VMEM] * 6)(
            star_pos, star_vel, star_radius, star_mdot, star_edot, star_yields
        )[0]
        all_stars = lax.all_gather(share, AXES, axis=0, tiled=True)
        all_star8, all_pay = all_stars[:, 0:8], all_stars[:, 8:32]

    with jax.named_scope("start"):
        send0, widths = call(
            start_kernel(cap, span),
            [((sent * 8, width), F32), ((nb + 1, width, width), F32)],
            [SMEM] + [VMEM] * 4,
            [pltpu.VMEM((nb, 8, width), F32)],
        )(asked, gas_pos, gas_vel, gas_mass, gas_smooth)
        far0 = swap(send0)
        list_c, list_slot, number = call(
            list_kernel(peers, cap, sb, nb, hits),
            [((whole,), i32), ((whole // GROUP,), i32), ((1,), i32)],
            [SMEM],
            [pltpu.SMEM((nb + 1,), i32)],
            smem_outs=range(3),
        )(asked)

    pos, vel, mass, energy, metals = gas_pos, gas_vel, gas_mass, gas_energy, gas_metals
    block3, block1 = ((nb, 3, width), F32), ((nb, width), F32)
    for substep in range(SUBSTEPS):
        first, last = substep == 0, substep == SUBSTEPS - 1
        with jax.named_scope("density"):
            far = [far0] if first else [far_pos, far_mv]
            sums, term, gain, density, send_gain = call(
                density_kernel(neighbours, cap, span, first),
                [((nb, 8, width), F32), block1, block1, block1, ((sent, width), F32)],
                [SMEM] * 2 + [VMEM] * (5 + len(far)),
                [pltpu.VMEM((nb, 1, width), F32)],
                work=heavy,
            )(asked, place, pos, vel, mass, gas_smooth, energy, *far)
            far_gain = swap(send_gain)
        with jax.named_scope("force"):
            far = [far0] if first else [far0, far_pos]
            outs = call(
                force_kernel(neighbours, cap, span, substep, first, last),
                [block3, block3, block1] + ([] if last else [((sent * 3, width), F32)]) + [((nb + 1, width, 48), BF16)],
                [SMEM] * 3 + [VMEM] * (8 + len(far)),
                [pltpu.SMEM((nb + TEAM,), i32)],
                work=heavy,
            )(asked, place, gas_bins, pos, vel, gas_smooth, energy, term, gain, sums, *far, far_gain)
            pos, vel, energy = outs[:3]
            sides = outs[-1]
        with jax.named_scope("omega"):
            part = call(
                omega_kernel(substep),
                [((stars, width), F32)],
                [SMEM] * 3 + [VMEM] * 3,
                [pltpu.VMEM((stars + 8, width), F32)],
                work=heavy,
            )(list_c, list_slot, number, sides, widths, all_star8)[0]
            total = swap(call(total_kernel(peers), [((stars, width), F32)], [VMEM])(swap(part))[0])
            if not last:
                total, send_pos = lax.optimization_barrier((total, outs[3]))
                far_pos = swap(send_pos)
        with jax.named_scope("deposit"):
            outs = call(
                deposit_kernel(substep, last, cap, span),
                [block1, block3, block1, ((nb, 16, width), F32)] + ([] if last else [((sent * 4, width), F32)]),
                [SMEM] * 4 + [VMEM] * 10,
                [pltpu.VMEM((nb + 1, width, 48), F32), pltpu.VMEM((nb, 4, width), F32)],
                work=heavy,
            )(asked, list_c, list_slot, number, sides, widths, all_star8, all_pay, total, mass, vel, energy, metals, density)
            mass, vel, energy, metals = outs[:4]
            if not last:
                send_mv, far_pos = lax.optimization_barrier((outs[4], far_pos))
                far_mv = swap(send_mv)
    return (pos, vel, mass, energy, metals)


def solution(mesh):
    split = [P(AXES, *([None] * (rank - 1))) for rank in (3, 3, 2, 2, 2, 3, 1, 2, 2, 3, 3, 2, 2, 2, 3, 2, 2)]
    return jax.shard_map(
        local,
        mesh=mesh,
        in_specs=tuple(split),
        out_specs=tuple(P(AXES, *([None] * (rank - 1))) for rank in (3, 3, 2, 2, 3)),
        check_vma=False,
    )
```
